32 devices in a mesh: rep: 8 (over y, x, core), shard: 4 (over z).
Axes of the slice: x: 2, y: 2, z: 4, core: 2. Of those that a mesh axis runs over, the one named last changes fastest.
Arguments:
- tokens: bfloat16 [16384, 1024], P(('rep', 'shard')), may hold values from -6 to 6
- doc_ids: int32 [16384], P(('rep', 'shard')), may hold values from 0 to 511, as said below
- routes: int32 [16384, 8], P(('rep', 'shard')), may hold values from 0 to 15, all different within a row; in each aligned block of 512 rows (0 to 511, 512 to 1023, ...) at most 288 rows name the same one
- norm_in_gain: bfloat16 [1024], P('shard'), may hold values from 0.5 to 1.5
- w_query: bfloat16 [1024, 1024], P('shard'), may hold values from -0.1875 to 0.1875
- w_key: bfloat16 [1024, 512], P('shard'), may hold values from -0.1875 to 0.1875
- w_value: bfloat16 [1024, 512], P('shard'), may hold values from -0.1875 to 0.1875
- w_out: bfloat16 [1024, 1024], P('shard'), may hold values from -0.75 to 0.75
- norm_mid_gain: bfloat16 [1024], P('shard'), may hold values from 0.5 to 1.5
- w_router: bfloat16 [1024, 16], P('shard'), may hold values from -0.09375 to 0.09375
- w_expert_in: bfloat16 [16, 1024, 1024], P('shard'), may hold values from -0.1875 to 0.1875
- w_expert_down: bfloat16 [16, 512, 1024], P('shard'), may hold values from -0.75 to 0.75
- cotangent: bfloat16 [16384, 1024], P(('rep', 'shard')), may hold values from -6 to 6
Outputs:
- mixed: bfloat16 [16384, 1024], P(('rep', 'shard'))
- grad_tokens: float32 [16384, 1024], P(('rep', 'shard'))
- grad_norm_in_gain: float32 [1024], P('shard')
- grad_w_query: float32 [1024, 1024], P('shard')
- grad_w_key: float32 [1024, 512], P('shard')
- grad_w_value: float32 [1024, 512], P('shard')
- grad_w_out: float32 [1024, 1024], P('shard')
- grad_norm_mid_gain: float32 [1024], P('shard')
- grad_w_router: float32 [1024, 16], P('shard')
- grad_w_expert_in: float32 [16, 1024, 1024], P('shard')
- grad_w_expert_down: float32 [16, 512, 1024], P('shard')
The draws below stay inside these ranges and needn't reach their ends.
Inputs may be any that keep to these rules, and one draw needn't show every extreme that they name: `doc_ids`: in every aligned block of 512 tokens the numbers start at 0 and rise by 0 or 1 from token to token. Among the 512 tokens of one device, no expert is named by more than 288 routes.
All inputs are finite; a program needn't handle non-finite values.
Results may differ from the reference program's by a relative error of at most 0.019.
Values may be sent and summed in bfloat16 or wider, within the bound.
A program may use at most 320 MiB of HBM per device.

```python
import math
import jax
import jax.numpy as jnp
import numpy as np
from jax import lax

D = 1024
HEADS = 16
KV_HEADS = 8
HEAD_DIM = 64
FF = 512
EXPERTS = 16
TOP_K = 8
TOK_DEV = 512
CAP = 288
TOKENS = 16384


def draw_doc_ids(key, part):
    block_count = TOKENS // TOK_DEV
    key_rate, key_single, key_many, key_bits = jax.random.split(key, 4)
    divisors = jnp.array([2, 8, 32, 128], dtype=jnp.int32)
    row_divisor = divisors[jax.random.randint(key_rate, (block_count,), 0, 4)]
    single_row = jax.random.randint(key_single, (), 0, block_count)
    many_row = (single_row + 1 + jax.random.randint(key_many, (), 0, block_count - 1)) % block_count
    row_index = jnp.arange(block_count, dtype=jnp.int32)
    row_divisor = jnp.where(row_index == many_row, 1, row_divisor)
    random_bits = jax.random.randint(key_bits, (block_count, TOK_DEV), 0, 1 << 20)
    place_row = jnp.arange(TOK_DEV, dtype=jnp.int32)[None, :]
    opening = (random_bits % row_divisor[:, None] == 0) | (place_row == 0)
    opening = jnp.where(row_index[:, None] == single_row, place_row == 0, opening)
    return (jnp.cumsum(opening.astype(jnp.int32), axis=1) - 1).astype(jnp.int32).reshape(-1)


def block_scale(own_key, dims, pieces, smallest, high):
    gain = 1.0
    for axis_at, parts in pieces:
        draws = jax.random.uniform(jax.random.fold_in(jax.random.fold_in(own_key, 6), axis_at), (parts,), jnp.float32, smallest / len(pieces), high / len(pieces))
        gain = gain * jnp.repeat(jnp.exp(draws), dims[axis_at] // parts).reshape((-1,) + (1,) * (len(dims) - 1 - axis_at))
    return gain


def routed_block(rng, own, number, rows, amount, top, reach, lean):
    order = jax.random.permutation(rng, amount)
    packed, usual = portions_of(amount, rows * top, reach, lean, True), portions_of(amount, rows * top, reach, lean, False)
    places = jnp.arange(amount)

    def named(tallies, turn):
        used = int((tallies > 0).sum())
        fixed = max(1, used // 4)
        shifted = fixed + (places - fixed + turn * (used - fixed)) % max(1, amount - fixed)
        return jnp.zeros((amount,), jnp.int32).at[order[jnp.where(places < fixed, places, shifted)]].set(jnp.asarray(tallies, jnp.int32))

    tallies = jnp.where(number % 4 == 0, named(packed, number // 4), named(usual, number - number // 4 - 1))
    mixed = jax.random.permutation(jax.random.fold_in(own, 3), amount)
    giver, sink = mixed[0:amount // 2 * 2:2], mixed[1:amount // 2 * 2:2]
    slack = jnp.minimum(tallies[giver] - 1, reach - tallies[sink]) // 2
    slack = jnp.where((giver == order[0]) | (sink == order[0]) | (tallies[sink] == 0), 0, jnp.maximum(slack, 0))
    shifted = jax.random.randint(jax.random.fold_in(own, 4), (amount // 2,), 0, 1 << 20) % (slack + 1)
    tallies = tallies.at[giver].add(-shifted).at[sink].add(shifted)
    items = jnp.searchsorted(jnp.cumsum(tallies), jnp.arange(rows * top), side="right").astype(jnp.int32)
    table = items.reshape(top, rows).T
    table = table[jax.random.permutation(jax.random.fold_in(own, 1), rows)]
    turn = jax.random.randint(jax.random.fold_in(own, 2), (rows, 1), 0, top)
    return jnp.take_along_axis(table, (jnp.arange(top)[None, :] + turn) % top, axis=1)


def portions_of(number_of, total, reach, skew, full):
    loads = [(1 << 20) // math.isqrt(rank ** skew) + 1 for rank in range(1, number_of + 1)]
    largest = reach if full else min(reach, max(-(-total // number_of), total * loads[0] // sum(loads)))
    least = 1 if total - largest >= number_of - 1 else 0
    counts, surplus = [largest] + [least] * (number_of - 1), total - largest - least * (number_of - 1)
    while surplus > 0:
        movable = [i for i in range(1, number_of) if counts[i] < largest] or [i for i in range(1, number_of) if counts[i] < reach]
        pool, budget = sum([loads[i] for i in movable]), surplus
        for i in movable:
            more = min(reach - counts[i], max(1, budget * loads[i] // pool), surplus)
            counts[i] = counts[i] + more
            surplus = surplus - more
    return np.array(counts)


def normal_values(rng, shape, deviation, bound, cuts=(), kind=jnp.bfloat16):
    level = block_scale(rng, shape, cuts, -0.22, 0.18) if cuts else 1.0
    result = jax.random.normal(rng, shape, jnp.float32) * deviation * level
    return jnp.minimum(jnp.maximum(result, -bound), bound).astype(kind)


def setup_inputs(seed: int = 0) -> dict:
    streams_of = jax.random.split(jax.random.key(seed), 14)
    tokens = normal_values(streams_of[0], (TOKENS, D), 1.0, 6.0, ((0, 32),))
    doc_ids = draw_doc_ids(jax.random.fold_in(streams_of[13], 71), 0)
    routes_keys = jax.random.split(jax.random.fold_in(streams_of[2], 1), TOKENS // TOK_DEV)
    routes_turns = jax.random.permutation(jax.random.fold_in(streams_of[2], 3), TOKENS // TOK_DEV)
    routes = jax.vmap(lambda own, number: routed_block(jax.random.fold_in(streams_of[2], 2), own, number, TOK_DEV, EXPERTS, TOP_K, CAP, 0))(routes_keys, routes_turns).reshape((TOKENS, TOP_K))
    norm_in_gain = jnp.clip(1.0 + 0.1 * jax.random.normal(streams_of[3], (D,), jnp.float32), 0.5, 1.5).astype(jnp.bfloat16)
    w_query = normal_values(streams_of[4], (D, HEADS * HEAD_DIM), D ** -0.5, 0.1875, ((0, 4),))
    w_key = normal_values(streams_of[5], (D, KV_HEADS * HEAD_DIM), D ** -0.5, 0.1875, ((0, 4),))
    w_value = normal_values(streams_of[6], (D, KV_HEADS * HEAD_DIM), D ** -0.5, 0.1875, ((0, 4),))
    w_out = normal_values(streams_of[7], (HEADS * HEAD_DIM, D), (D // 16) ** -0.5, 0.75, ((0, 4),))
    norm_mid_gain = jnp.clip(1.0 + 0.1 * jax.random.normal(streams_of[8], (D,), jnp.float32), 0.5, 1.5).astype(jnp.bfloat16)
    w_router = normal_values(streams_of[9], (D, EXPERTS), (4 * D) ** -0.5, 0.09375, ((0, 4),))
    w_expert_in = normal_values(streams_of[10], (EXPERTS, D, 2 * FF), D ** -0.5, 0.1875, ((0, 4),))
    w_expert_down = normal_values(streams_of[11], (EXPERTS, FF, D), (FF // 8) ** -0.5, 0.75, ((0, 4),))
    cotangent = normal_values(streams_of[12], (TOKENS, D), 1.0, 6.0, ((0, 32),))
    return {"tokens": tokens, "doc_ids": doc_ids, "routes": routes, "norm_in_gain": norm_in_gain, "w_query": w_query, "w_key": w_key, "w_value": w_value, "w_out": w_out, "norm_mid_gain": norm_mid_gain, "w_router": w_router, "w_expert_in": w_expert_in, "w_expert_down": w_expert_down, "cotangent": cotangent}


highest = lax.Precision.HIGHEST
epsilon = 1e-06
rope_base = 10000.0
masked_score = -1e+30

@jax.custom_vjp
def low(v):
    return lax.optimization_barrier(v.astype(jnp.bfloat16)).astype(jnp.float32)

@jax.custom_vjp
def low_back(v):
    return v

def low_keep(v):
    return (low(v), None)

def low_pass(kept, grad):
    return (grad,)

def back_keep(v):
    return (v, None)

def back_low(kept, grad):
    return (low(grad),)
low.defvjp(low_keep, low_pass)
low_back.defvjp(back_keep, back_low)

def positions(doc_rows):
    row_count = doc_rows.shape[0]
    places = jnp.arange(row_count, dtype=jnp.int32)
    opening = jnp.concatenate([jnp.ones((1,), dtype=jnp.bool_), doc_rows[1:] != doc_rows[:-1]])
    begins = lax.cummax(jnp.where(opening, places, 0), axis=0)
    return (places - begins).astype(jnp.int32)

def rotary_tables(places, head_width):
    half_width = head_width // 2
    frequencies = jnp.power(rope_base, -2.0 * jnp.arange(half_width, dtype=jnp.float32) / head_width)
    angles = places.astype(jnp.float32)[:, None] * frequencies[None, :]
    return (jnp.cos(angles)[:, None, :], jnp.sin(angles)[:, None, :])

def rotate(values, cosine, sine_table):
    half_width = values.shape[-1] // 2
    former, latter = (values[..., :half_width], values[..., half_width:])
    return jnp.concatenate([former * cosine - latter * sine_table, latter * cosine + former * sine_table], axis=-1)

def rms_scale(values):
    return lax.rsqrt(lax.optimization_barrier(jnp.mean(values * values, axis=-1, keepdims=True)) + epsilon)

def dispatch(route_rows):
    flat_routes = route_rows.reshape(-1)
    route_count = flat_routes.shape[0]
    onehot = (flat_routes[:, None] == jnp.arange(EXPERTS, dtype=jnp.int32)[None, :]).astype(jnp.int32)
    expert_rank = lax.optimization_barrier(jnp.sum((jnp.cumsum(onehot, axis=0) - 1) * onehot, axis=1))
    slot_index = (flat_routes * CAP + expert_rank).astype(jnp.int32)
    source = jnp.full((EXPERTS * CAP,), route_count, dtype=jnp.int32).at[slot_index].set(jnp.arange(route_count, dtype=jnp.int32))
    filled = source < route_count
    token_of = jnp.where(filled, source // TOP_K, 0).astype(jnp.int32)
    route_of = jnp.where(filled, source, 0).astype(jnp.int32)
    return (token_of, route_of, filled)

def layer_block(params, inputs, doc_rows, route_rows):
    gain_in, query_w, key_w, value_w, out_w, gain_mid, router_w, expert_in_w, expert_down_w = params
    row_count = inputs.shape[0]
    groups = HEADS // KV_HEADS
    cosine, sine_table = rotary_tables(positions(doc_rows), HEAD_DIM)
    first = low(inputs * rms_scale(inputs) * gain_in)
    query_pre = low_back(jnp.dot(first, query_w, precision=highest))
    key_pre = low_back(jnp.dot(first, key_w, precision=highest))
    value_rows = low(low_back(jnp.dot(first, value_w, precision=highest))).reshape(row_count, KV_HEADS, HEAD_DIM)
    query_rows = low(rotate(query_pre.reshape(row_count, HEADS, HEAD_DIM), cosine, sine_table)).reshape(row_count, KV_HEADS, groups, HEAD_DIM)
    key_rows = low(rotate(key_pre.reshape(row_count, KV_HEADS, HEAD_DIM), cosine, sine_table))
    scores = jnp.einsum('qgrd,kgd->grqk', query_rows, key_rows, precision=highest) * HEAD_DIM ** (-0.5)
    places = jnp.arange(row_count, dtype=jnp.int32)
    allowed = (doc_rows[:, None] == doc_rows[None, :]) & (places[:, None] >= places[None, :])
    scores = low_back(jnp.where(allowed, scores, masked_score))
    row_max = lax.optimization_barrier(jnp.max(scores, axis=-1, keepdims=True))
    exponent = jnp.exp(scores - row_max)
    probs = exponent / lax.optimization_barrier(jnp.sum(exponent, axis=-1, keepdims=True))
    attended = jnp.einsum('grqk,kgd->qgrd', low(probs), value_rows, precision=highest).reshape(row_count, HEADS * HEAD_DIM)
    attended = low_back(low(attended))
    middle = inputs + low_back(jnp.dot(attended, out_w, precision=highest))
    second = low(middle * rms_scale(middle) * gain_mid)
    logits = low_back(jnp.dot(second, router_w, precision=highest))
    chosen = jnp.take_along_axis(logits, route_rows, axis=1)
    chosen_max = lax.optimization_barrier(jnp.max(chosen, axis=1, keepdims=True))
    gate_exp = jnp.exp(chosen - chosen_max)
    gates = gate_exp / lax.optimization_barrier(jnp.sum(gate_exp, axis=1, keepdims=True))
    token_of, route_of, filled = dispatch(route_rows)
    fill_mask = filled.astype(jnp.float32)
    expert_rows = (second[token_of] * fill_mask[:, None]).reshape(EXPERTS, CAP, D)
    both_parts = low_back(jnp.einsum('ecd,edf->ecf', expert_rows, expert_in_w, precision=highest))
    hidden = low(jax.nn.silu(both_parts[..., :FF]) * both_parts[..., FF:])
    expert_out = low_back(jnp.einsum('ecf,efd->ecd', hidden, expert_down_w, precision=highest)).reshape(EXPERTS * CAP, D)
    slot_gates = gates.reshape(-1)[route_of] * fill_mask
    combined = jax.ops.segment_sum(expert_out * slot_gates[:, None], token_of, num_segments=row_count)
    return middle + combined

def reference(tokens, doc_ids, routes, norm_in_gain, w_query, w_key, w_value, w_out, norm_mid_gain, w_router, w_expert_in, w_expert_down, cotangent):
    block_count = tokens.shape[0] // TOK_DEV
    params = (norm_in_gain.astype(jnp.float32), w_query.astype(jnp.float32), w_key.astype(jnp.float32), w_value.astype(jnp.float32), w_out.astype(jnp.float32), norm_mid_gain.astype(jnp.float32), w_router.astype(jnp.float32), w_expert_in.astype(jnp.float32), w_expert_down.astype(jnp.float32))
    inputs = tokens.astype(jnp.float32).reshape(block_count, TOK_DEV, D)
    doc_blocks = doc_ids.reshape(block_count, TOK_DEV)
    route_blocks = routes.reshape(block_count, TOK_DEV, TOP_K)

    def forward(weights_all, inputs_all):

        def one_block(block_items):
            return layer_block(weights_all, block_items[0], block_items[1], block_items[2])
        return lax.map(jax.checkpoint(one_block), (inputs_all, doc_blocks, route_blocks))
    outputs, pullback = jax.vjp(forward, params, inputs)
    grad_params, grad_inputs = pullback(cotangent.astype(jnp.float32).reshape(block_count, TOK_DEV, D))
    return (outputs.reshape(-1, D).astype(jnp.bfloat16), grad_inputs.reshape(-1, D), grad_params[0], grad_params[1], grad_params[2], grad_params[3], grad_params[4], grad_params[5], grad_params[6], grad_params[7], grad_params[8])
```

```python
import jax
import jax.numpy as jnp
from jax import lax
from jax.sharding import PartitionSpec as P

HEADS = 16
KV_HEADS = 8
HEAD_DIM = 64
EXPERTS = 16
PAD = 128


epsilon = 1e-06
rope_base = 10000.0
masked_score = -1e30


def positions(doc_rows):
    row_count = doc_rows.shape[0]
    places = jnp.arange(row_count, dtype=jnp.int32)
    opening = jnp.concatenate([jnp.ones((1,), dtype=jnp.bool_), doc_rows[1:] != doc_rows[:-1]])
    begins = lax.cummax(jnp.where(opening, places, 0), axis=0)
    return places - begins


def rotary_tables(places, head_width):
    half_width = head_width // 2
    frequencies = jnp.power(
        rope_base, -2.0 * jnp.arange(half_width, dtype=jnp.float32) / head_width
    )
    angles = places.astype(jnp.float32)[:, None] * frequencies[None, :]
    return (jnp.cos(angles)[:, None, :], jnp.sin(angles)[:, None, :])


def rotate(values, cosine, sine_table):
    half_width = values.shape[-1] // 2
    former, latter = (values[..., :half_width], values[..., half_width:])
    return jnp.concatenate(
        [former * cosine - latter * sine_table, latter * cosine + former * sine_table], axis=-1
    )


def unrotate(values, cosine, sine_table):
    half_width = values.shape[-1] // 2
    former, latter = (values[..., :half_width], values[..., half_width:])
    return jnp.concatenate(
        [former * cosine + latter * sine_table, latter * cosine - former * sine_table], axis=-1
    )


def normalize(values):
    row_scale = lax.rsqrt(jnp.mean(values * values, axis=-1, keepdims=True) + epsilon)
    return (values * row_scale, row_scale)


def norm_back(grad_scaled, normed, row_scale, gain_full):
    grad_normed = grad_scaled * gain_full
    inner = jnp.mean(grad_normed * normed, axis=-1, keepdims=True)
    return (row_scale * (grad_normed - normed * inner), jnp.sum(grad_scaled * normed, axis=0))


def score_block(query_blk, key_part, doc_query, doc_key):
    scores = jnp.einsum(
        "qgrd,kgd->grqk", query_blk, key_part, preferred_element_type=jnp.float32
    ) * query_blk.shape[-1] ** (-0.5)
    query_place = jnp.arange(query_blk.shape[0], dtype=jnp.int32)
    key_place = jnp.arange(key_part.shape[0], dtype=jnp.int32)
    allowed = (doc_query[:, None] == doc_key[None, :]) & (
        query_place[:, None] >= key_place[None, :]
    )
    return jnp.where(allowed, scores, masked_score)


def attend(query_rows, key_rows, value_rows, doc_rows):
    scores = score_block(query_rows, key_rows, doc_rows, doc_rows)
    row_max = jnp.max(scores, axis=-1, keepdims=True)
    exponent = jnp.exp(scores - row_max)
    row_total = jnp.sum(exponent, axis=-1, keepdims=True)
    probs_low = (exponent / row_total).astype(jnp.bfloat16)
    outputs = jnp.einsum(
        "grqk,kgd->qgrd", probs_low, value_rows, preferred_element_type=jnp.float32
    ).astype(jnp.bfloat16)
    lse_parts = row_max + jnp.log(row_total)
    return (outputs, lse_parts)


def attend_back(query_rows, key_rows, value_rows, doc_rows, log_sums, grad_att):
    row_count = query_rows.shape[0]
    block_rows = min(512, row_count)
    scale_factor = query_rows.shape[-1] ** (-0.5)
    grad_key = jnp.zeros(key_rows.shape, jnp.float32)
    grad_value = jnp.zeros(value_rows.shape, jnp.float32)
    scores = score_block(query_rows, key_rows, doc_rows, doc_rows)
    probs = jnp.exp(scores - log_sums)
    grad_probs = jnp.einsum(
        "qgrd,kgd->grqk", grad_att, value_rows, preferred_element_type=jnp.float32
    )
    inner = jnp.sum(probs * grad_probs, axis=-1, keepdims=True)
    grad_scores = (probs * (grad_probs - inner)).astype(jnp.bfloat16)
    query_parts = (
        jnp.einsum("grqk,kgd->qgrd", grad_scores, key_rows, preferred_element_type=jnp.float32)
        * scale_factor
    )
    grad_key = grad_key.at[:block_rows].add(
        jnp.einsum("grqk,qgrd->kgd", grad_scores, query_rows, preferred_element_type=jnp.float32)
        * scale_factor
    )
    grad_value = grad_value.at[:block_rows].add(
        jnp.einsum(
            "grqk,qgrd->kgd",
            probs.astype(jnp.bfloat16),
            grad_att,
            preferred_element_type=jnp.float32,
        )
    )
    return (query_parts, grad_key, grad_value)


def gather_shard(piece):
    return lax.all_gather(piece, "shard", axis=0, tiled=True)


def shards(
    tokens,
    doc_ids,
    routes,
    norm_in_gain,
    w_query,
    w_key,
    w_value,
    w_out,
    norm_mid_gain,
    w_router,
    w_expert_in,
    w_expert_down,
    cotangent,
):
    bf16, f32 = jnp.bfloat16, jnp.float32
    row_count, model_width = tokens.shape
    groups = HEADS // KV_HEADS
    query_cols = w_query.shape[1]
    kv_cols = w_key.shape[1]
    own_rows = w_query.shape[0]
    own_experts, ff = w_expert_down.shape[:2]
    shard_at = lax.axis_index("shard")

    small = jnp.concatenate(
        [
            w_router,
            norm_in_gain[:, None],
            norm_mid_gain[:, None],
            jnp.zeros((own_rows, PAD - EXPERTS - 2), bf16),
        ],
        axis=1,
    )
    qkv_full = gather_shard(jnp.concatenate([w_query, w_key, w_value, small], axis=1))
    qkv_w = qkv_full[:, : query_cols + 2 * kv_cols]
    small_full = qkv_full[:, query_cols + 2 * kv_cols :]
    router_full = small_full[:, :EXPERTS]
    gain_in = small_full[:, EXPERTS].astype(f32)
    gain_mid = small_full[:, EXPERTS + 1].astype(f32)
    out_w = gather_shard(w_out)
    mask_own = jnp.any(
        routes[:, :, None] == jnp.arange(EXPERTS, dtype=jnp.int32)[None, None, :], axis=1
    )
    side = jnp.concatenate(
        [cotangent, mask_own.astype(bf16), jnp.zeros((row_count, PAD - EXPERTS), bf16)], axis=1
    )
    side_all = gather_shard(side)
    dy_all = side_all[:, :model_width]
    mask_all = side_all[:, model_width : model_width + EXPERTS] > 0

    inputs = tokens.astype(f32)
    grad_final = cotangent.astype(f32)
    cosine, sine_table = rotary_tables(positions(doc_ids), HEAD_DIM)
    normed_in, scale_in = normalize(inputs)
    first_low = (normed_in * gain_in).astype(bf16)
    qkv_pre = jnp.dot(first_low, qkv_w, preferred_element_type=f32)
    query_pre = qkv_pre[:, :query_cols]
    key_pre = qkv_pre[:, query_cols : query_cols + kv_cols]
    value_pre = qkv_pre[:, query_cols + kv_cols :]
    query_rows = (
        rotate(query_pre.reshape(row_count, HEADS, HEAD_DIM), cosine, sine_table)
        .astype(bf16)
        .reshape(row_count, KV_HEADS, groups, HEAD_DIM)
    )
    key_rows = rotate(key_pre.reshape(row_count, KV_HEADS, HEAD_DIM), cosine, sine_table).astype(
        bf16
    )
    value_rows = value_pre.astype(bf16).reshape(row_count, KV_HEADS, HEAD_DIM)
    att_rows, log_sums = attend(query_rows, key_rows, value_rows, doc_ids)
    att_low = att_rows.reshape(row_count, query_cols)
    middle = inputs + jnp.dot(att_low, out_w, preferred_element_type=f32)
    normed_mid, scale_mid = normalize(middle)
    second_low = (normed_mid * gain_mid).astype(bf16)

    second_all = gather_shard(second_low)
    logits = jnp.dot(second_all, router_full, preferred_element_type=f32)
    chosen = jnp.where(mask_all, logits, masked_score)
    gate_exp = jnp.where(mask_all, jnp.exp(chosen - jnp.max(chosen, axis=1, keepdims=True)), 0.0)
    gates_all = gate_exp / jnp.sum(gate_exp, axis=1, keepdims=True)
    gates_here = lax.dynamic_slice_in_dim(gates_all, shard_at * own_experts, own_experts, axis=1)
    gates_own = lax.dynamic_slice_in_dim(gates_all, shard_at * row_count, row_count, axis=0)

    gated, grad_both, grad_gates_here = experts(
        second_all, dy_all, gates_here, w_expert_in, w_expert_down
    )
    combined = jnp.einsum("etf,efd->td", gated, w_expert_down, preferred_element_type=f32)
    combined_own = lax.psum_scatter(
        combined.astype(bf16), "shard", scatter_dimension=0, tiled=True
    )
    grad_second_here = jnp.einsum("etf,edf->td", grad_both, w_expert_in, preferred_element_type=f32)
    gate_cols = lax.dynamic_update_slice_in_dim(
        jnp.zeros((grad_gates_here.shape[0], EXPERTS), f32),
        grad_gates_here,
        shard_at * own_experts,
        axis=1,
    )
    gate_high = gate_cols.astype(bf16)
    gate_low = (gate_cols - gate_high.astype(f32)).astype(bf16)
    back_rows = jnp.concatenate(
        [
            grad_second_here.astype(bf16),
            gate_high,
            gate_low,
            jnp.zeros((gate_cols.shape[0], PAD - 2 * EXPERTS), bf16),
        ],
        axis=1,
    )
    back_own = lax.psum_scatter(back_rows, "shard", scatter_dimension=0, tiled=True)
    grad_in_here = jnp.einsum("td,etf->edf", second_all, grad_both, preferred_element_type=f32)
    grad_down_here = jnp.einsum("etf,td->efd", gated, dy_all, preferred_element_type=f32)
    grad_in_own = lax.psum(grad_in_here.astype(bf16), "rep").astype(f32)
    grad_down_own = lax.psum(grad_down_here.astype(bf16), "rep").astype(f32)

    mixed = (middle + combined_own.astype(f32)).astype(bf16)
    gate_back = back_own[:, model_width : model_width + 2 * EXPERTS].astype(f32)
    grad_gates = gate_back[:, :EXPERTS] + gate_back[:, EXPERTS:]
    grad_logits = (
        gates_own * (grad_gates - jnp.sum(gates_own * grad_gates, axis=1, keepdims=True))
    ).astype(bf16)
    grad_router = jnp.einsum("td,te->de", second_low, grad_logits, preferred_element_type=f32)
    grad_second = back_own[:, :model_width].astype(f32) + jnp.einsum(
        "te,de->td", grad_logits, router_full, preferred_element_type=f32
    )
    grad_mid_norm, grad_gain_mid = norm_back(grad_second, normed_mid, scale_mid, gain_mid)
    grad_middle = grad_final + grad_mid_norm
    grad_branch = grad_middle.astype(bf16)
    grad_out_w = jnp.einsum("ta,td->ad", att_low, grad_branch, preferred_element_type=f32)
    grad_att = jnp.einsum("td,ad->ta", grad_branch, out_w, preferred_element_type=f32).astype(bf16)
    grad_query_rot, grad_key_rot, grad_value_rows = attend_back(
        query_rows,
        key_rows,
        value_rows,
        doc_ids,
        log_sums,
        grad_att.reshape(row_count, KV_HEADS, groups, HEAD_DIM),
    )
    grad_query_pre = (
        unrotate(grad_query_rot.reshape(row_count, HEADS, HEAD_DIM), cosine, sine_table)
        .astype(bf16)
        .reshape(row_count, query_cols)
    )
    grad_key_pre = unrotate(grad_key_rot, cosine, sine_table).astype(bf16)
    grad_pre = jnp.concatenate(
        [
            grad_query_pre,
            grad_key_pre.reshape(row_count, kv_cols),
            grad_value_rows.astype(bf16).reshape(row_count, kv_cols),
        ],
        axis=1,
    )
    grad_qkv = jnp.einsum("td,tc->dc", first_low, grad_pre, preferred_element_type=f32)
    columns = jnp.einsum("tc,dc->td", grad_pre, qkv_w, preferred_element_type=f32)
    grad_in_norm, grad_gain_in = norm_back(columns, normed_in, scale_in, gain_in)
    grad_tokens = grad_middle + grad_in_norm

    joint = jnp.concatenate(
        [
            grad_qkv.astype(bf16),
            grad_out_w.astype(bf16),
            grad_router.astype(bf16),
            grad_gain_in.astype(bf16)[:, None],
            grad_gain_mid.astype(bf16)[:, None],
            jnp.zeros((model_width, PAD - EXPERTS - 2), bf16),
        ],
        axis=1,
    )
    joint_own = reduce_joint(joint).astype(f32)
    edges = [0]
    for width in (query_cols, kv_cols, kv_cols, w_out.shape[1], EXPERTS, 1, 1):
        edges.append(edges[-1] + width)
    pieces = [joint_own[:, a:b] for a, b in zip(edges[:-1], edges[1:])]
    query_own, key_own, value_own, out_own, router_own, gain_in_own, gain_mid_own = pieces
    return (
        mixed,
        grad_tokens,
        gain_in_own[:, 0],
        query_own,
        key_own,
        value_own,
        out_own,
        gain_mid_own[:, 0],
        router_own,
        grad_in_own,
        grad_down_own,
    )


def reduce_joint(joint):
    part = lax.psum_scatter(joint, "shard", scatter_dimension=0, tiled=True)
    return lax.psum(part, "rep")


def experts(rows, dy_rows, gates, in_w, down_w):
    f32, bf16 = jnp.float32, jnp.bfloat16
    both = jnp.einsum("td,edf->etf", rows, in_w, preferred_element_type=f32)
    half_width = both.shape[-1] // 2
    gate_part, up_part = (both[..., :half_width], both[..., half_width:])
    sigmoid_gate = jax.nn.sigmoid(gate_part)
    silu_gate = gate_part * sigmoid_gate
    hidden = (silu_gate * up_part).astype(bf16).astype(f32)
    back = jnp.einsum("td,efd->etf", dy_rows, down_w, preferred_element_type=f32)
    gate_cols = gates.T[:, :, None]
    grad_gates = jnp.sum(hidden * back, axis=-1).T
    gated = (hidden * gate_cols).astype(bf16)
    grad_hidden = back * gate_cols
    grad_gate = grad_hidden * up_part * sigmoid_gate * (1.0 + gate_part * (1.0 - sigmoid_gate))
    grad_both = jnp.concatenate([grad_gate, grad_hidden * silu_gate], axis=-1).astype(bf16)
    return (gated, grad_both, grad_gates)


def solution(mesh):
    in_specs = (
        P(("rep", "shard"), None),
        P(("rep", "shard")),
        P(("rep", "shard"), None),
        P("shard"),
        P("shard", None),
        P("shard", None),
        P("shard", None),
        P("shard", None),
        P("shard"),
        P("shard", None),
        P("shard", None, None),
        P("shard", None, None),
        P(("rep", "shard"), None),
    )
    out_specs = (
        P(("rep", "shard"), None),
        P(("rep", "shard"), None),
        P("shard"),
        P("shard", None),
        P("shard", None),
        P("shard", None),
        P("shard", None),
        P("shard"),
        P("shard", None),
        P("shard", None, None),
        P("shard", None, None),
    )
    return jax.shard_map(shards, mesh=mesh, in_specs=in_specs, out_specs=out_specs, check_vma=False)
```

```python
import jax
import jax.numpy as jnp
from jax import lax
from jax.experimental import pallas as pl
from jax.experimental.pallas import tpu as pltpu
from jax.sharding import PartitionSpec as P

HEADS = 16
KV_HEADS = 8
HEAD_DIM = 64
EXPERTS = 16
PAD = 128
VMEM_BYTES = 54 * 2**20


epsilon = 1e-06
rope_base = 10000.0
masked_score = -1e30


def positions(doc_rows):
    row_count = doc_rows.shape[0]
    places = jnp.arange(row_count, dtype=jnp.int32)
    opening = jnp.concatenate([jnp.ones((1,), dtype=jnp.bool_), doc_rows[1:] != doc_rows[:-1]])
    begins = lax.cummax(jnp.where(opening, places, 0), axis=0)
    return places - begins


def rotary_tables(places, head_width):
    half_width = head_width // 2
    frequencies = jnp.power(
        rope_base, -2.0 * jnp.arange(half_width, dtype=jnp.float32) / head_width
    )
    angles = places.astype(jnp.float32)[:, None] * frequencies[None, :]
    return (jnp.cos(angles)[:, None, :], jnp.sin(angles)[:, None, :])


def rotate(values, cosine, sine_table):
    half_width = values.shape[-1] // 2
    former, latter = (values[..., :half_width], values[..., half_width:])
    return jnp.concatenate(
        [former * cosine - latter * sine_table, latter * cosine + former * sine_table], axis=-1
    )


def unrotate(values, cosine, sine_table):
    half_width = values.shape[-1] // 2
    former, latter = (values[..., :half_width], values[..., half_width:])
    return jnp.concatenate(
        [former * cosine + latter * sine_table, latter * cosine - former * sine_table], axis=-1
    )


def normalize(values):
    row_scale = lax.rsqrt(jnp.mean(values * values, axis=-1, keepdims=True) + epsilon)
    return (values * row_scale, row_scale)


def norm_back(grad_scaled, normed, row_scale, gain_full):
    grad_normed = grad_scaled * gain_full
    inner = jnp.mean(grad_normed * normed, axis=-1, keepdims=True)
    return (row_scale * (grad_normed - normed * inner), jnp.sum(grad_scaled * normed, axis=0))


def score_block(query_blk, key_part, doc_query, doc_key):
    scores = jnp.einsum(
        "qgrd,kgd->grqk", query_blk, key_part, preferred_element_type=jnp.float32
    ) * query_blk.shape[-1] ** (-0.5)
    query_place = jnp.arange(query_blk.shape[0], dtype=jnp.int32)
    key_place = jnp.arange(key_part.shape[0], dtype=jnp.int32)
    allowed = (doc_query[:, None] == doc_key[None, :]) & (
        query_place[:, None] >= key_place[None, :]
    )
    return jnp.where(allowed, scores, masked_score)


def attend(query_rows, key_rows, value_rows, doc_rows):
    scores = score_block(query_rows, key_rows, doc_rows, doc_rows)
    row_max = jnp.max(scores, axis=-1, keepdims=True)
    exponent = jnp.exp(scores - row_max)
    row_total = jnp.sum(exponent, axis=-1, keepdims=True)
    probs_low = (exponent / row_total).astype(jnp.bfloat16)
    outputs = jnp.einsum(
        "grqk,kgd->qgrd", probs_low, value_rows, preferred_element_type=jnp.float32
    ).astype(jnp.bfloat16)
    lse_parts = row_max + jnp.log(row_total)
    return (outputs, lse_parts)


def attend_back(query_rows, key_rows, value_rows, doc_rows, log_sums, grad_att):
    row_count = query_rows.shape[0]
    block_rows = min(512, row_count)
    scale_factor = query_rows.shape[-1] ** (-0.5)
    grad_key = jnp.zeros(key_rows.shape, jnp.float32)
    grad_value = jnp.zeros(value_rows.shape, jnp.float32)
    scores = score_block(query_rows, key_rows, doc_rows, doc_rows)
    probs = jnp.exp(scores - log_sums)
    grad_probs = jnp.einsum(
        "qgrd,kgd->grqk", grad_att, value_rows, preferred_element_type=jnp.float32
    )
    inner = jnp.sum(probs * grad_probs, axis=-1, keepdims=True)
    grad_scores = (probs * (grad_probs - inner)).astype(jnp.bfloat16)
    query_parts = (
        jnp.einsum("grqk,kgd->qgrd", grad_scores, key_rows, preferred_element_type=jnp.float32)
        * scale_factor
    )
    grad_key = grad_key.at[:block_rows].add(
        jnp.einsum("grqk,qgrd->kgd", grad_scores, query_rows, preferred_element_type=jnp.float32)
        * scale_factor
    )
    grad_value = grad_value.at[:block_rows].add(
        jnp.einsum(
            "grqk,qgrd->kgd",
            probs.astype(jnp.bfloat16),
            grad_att,
            preferred_element_type=jnp.float32,
        )
    )
    return (query_parts, grad_key, grad_value)


MESH = pl.DeviceIdType.MESH
HALVES = 2


def bit_orders(reps):
    bits = reps.bit_length() - 1
    first = list(range(bits))
    return (first, first[:1] + first[1:][::-1])


def rep_place(rep_at, order):
    place = 0
    for bit in order:
        place = place * 2 + rep_at // 2**bit % 2
    return place


def partner(rep_at, bit):
    return rep_at + 2**bit * (1 - 2 * (rep_at // 2**bit % 2))


def halves_of(columns):
    tiles = columns // 128
    left = (tiles + 1) // 2 * 128
    return (pl.ds(0, left), pl.ds(left, columns - left))


def meet(rep_at, shard_at, reps, shard_count):
    barrier = pltpu.get_barrier_semaphore()
    bits = reps.bit_length() - 1
    for bit in range(bits):
        pl.semaphore_signal(
            barrier, inc=1, device_id=(partner(rep_at, bit), shard_at), device_id_type=MESH
        )
    for step in range(1, shard_count):
        pl.semaphore_signal(
            barrier,
            inc=1,
            device_id=(rep_at, (shard_at + step) % shard_count),
            device_id_type=MESH,
        )
    pl.semaphore_wait(barrier, bits + shard_count - 1)


def spread(out, orders, columns, rep_at, shard_at, sends, recvs):
    bits = len(orders[0])
    flying = [None] * HALVES
    for at in reversed(range(bits)):
        window = 2 ** (bits - 1 - at)
        for half in range(HALVES):
            order = orders[half]
            place = rep_place(rep_at, order)
            begin = place // window * window
            if flying[half] is not None:
                flying[half].wait()
            block = out.at[:, pl.ds(begin, window), :, columns[half]]
            flying[half] = pltpu.make_async_remote_copy(
                src_ref=block,
                dst_ref=block,
                send_sem=sends.at[half, at],
                recv_sem=recvs.at[half, at],
                device_id=(partner(rep_at, order[at]), shard_at),
                device_id_type=MESH,
            )
            flying[half].start()
    for half in range(HALVES):
        flying[half].wait()


def gather_kernel(reps, shard_count, piece, out, z_send, z_recv, sends, recvs):
    rep_at, shard_at = (lax.axis_index("rep"), lax.axis_index("shard"))
    orders = bit_orders(reps)
    columns = halves_of(piece.shape[-1])
    meet(rep_at, shard_at, reps, shard_count)
    flying = []
    for half in range(HALVES):
        place = rep_place(rep_at, orders[half])
        for step in range(1, shard_count):
            copy = pltpu.make_async_remote_copy(
                src_ref=piece.at[place, :, columns[half]],
                dst_ref=out.at[shard_at, place, :, columns[half]],
                send_sem=z_send.at[half, step - 1],
                recv_sem=z_recv.at[half, step - 1],
                device_id=(rep_at, (shard_at + step) % shard_count),
                device_id_type=MESH,
            )
            copy.start()
            flying.append(copy)
        out[shard_at, place, :, columns[half]] = piece[place, :, columns[half]]
    for copy in flying:
        copy.wait()
    spread(out, orders, columns, rep_at, shard_at, sends, recvs)


def gather_all(piece, reps, shard_count, number):
    own, width = piece.shape
    rows = own // reps
    bits = reps.bit_length() - 1
    out = pl.pallas_call(
        lambda *refs: gather_kernel(reps, shard_count, *refs),
        out_shape=jax.ShapeDtypeStruct((shard_count, reps, rows, width), piece.dtype),
        in_specs=[pl.BlockSpec(memory_space=pltpu.VMEM)],
        out_specs=pl.BlockSpec(memory_space=pltpu.VMEM),
        scratch_shapes=[
            pltpu.SemaphoreType.DMA((HALVES, shard_count)),
            pltpu.SemaphoreType.DMA((HALVES, shard_count)),
            pltpu.SemaphoreType.DMA((HALVES, bits)),
            pltpu.SemaphoreType.DMA((HALVES, bits)),
        ],
        compiler_params=pltpu.CompilerParams(
            collective_id=number, has_side_effects=True, vmem_limit_bytes=VMEM_BYTES
        ),
        cost_estimate=pl.CostEstimate(
            flops=0, bytes_accessed=16 * shard_count * own * width, transcendentals=0
        ),
    )(piece.reshape(reps, rows, width))
    return out.reshape(shard_count * own, width)


def reduce_kernel(reps, shard_count, parts, out, *scratch):
    bits = reps.bit_length() - 1
    f32 = jnp.float32
    landed = [scratch[half * bits : (half + 1) * bits] for half in range(HALVES)]
    rest = scratch[HALVES * bits :]
    if shard_count > 1:
        z_land, (z_send, z_recv) = (rest[:HALVES], rest[HALVES : HALVES + 2])
        rest = rest[HALVES + 2 :]
    r_send, r_recv, sends, recvs = rest
    rep_at, shard_at = (lax.axis_index("rep"), lax.axis_index("shard"))
    orders = bit_orders(reps)
    columns = halves_of(parts.shape[-1])
    meet(rep_at, shard_at, reps, shard_count)
    flying = [None] * HALVES

    def source(half, at):
        return parts.at[:, :, :, columns[half]] if at == 0 else landed[half][at - 1]

    def begin(half, at):
        bit = orders[half][at]
        many = reps // 2 ** (at + 1)
        away = (1 - rep_at // 2**bit % 2) * many
        flying[half] = pltpu.make_async_remote_copy(
            src_ref=source(half, at).at[:, pl.ds(away, many)],
            dst_ref=landed[half][at],
            send_sem=r_send.at[half, at],
            recv_sem=r_recv.at[half, at],
            device_id=(partner(rep_at, bit), shard_at),
            device_id_type=MESH,
        )
        flying[half].start()

    for half in range(HALVES):
        begin(half, 0)
    for at in range(bits):
        many = reps // 2 ** (at + 1)
        for half in range(HALVES):
            flying[half].wait()
            keep = rep_at // 2 ** orders[half][at] % 2 * many
            mine, came = (source(half, at), landed[half][at])

            @pl.loop(0, parts.shape[0] * many)
            def _(index):
                outer, inner = (index // many, index % many)
                came[outer, inner] = (
                    came[outer, inner].astype(f32) + mine[outer, keep + inner].astype(f32)
                ).astype(came.dtype)

            if at + 1 < bits:
                begin(half, at + 1)
    copies = []
    if shard_count > 1:
        for half in range(HALVES):
            for step in range(1, shard_count):
                to = (shard_at + step) % shard_count
                copy = pltpu.make_async_remote_copy(
                    src_ref=landed[half][-1].at[to, 0],
                    dst_ref=z_land[half].at[step - 1],
                    send_sem=z_send.at[half, step - 1],
                    recv_sem=z_recv.at[half, step - 1],
                    device_id=(rep_at, to),
                    device_id_type=MESH,
                )
                copy.start()
                copies.append(copy)
    for copy in copies:
        copy.wait()
    for half in range(HALVES):
        place = rep_place(rep_at, orders[half])
        if shard_count > 1:
            total = landed[half][-1][shard_at, 0].astype(f32)
            for step in range(1, shard_count):
                total = total + z_land[half][step - 1].astype(f32)
            out[0, place, :, columns[half]] = total.astype(out.dtype)
        else:
            out[0, place, :, columns[half]] = landed[half][-1][0, 0]
    spread(out, orders, columns, rep_at, shard_at, sends, recvs)


def reduce_all(parts, reps, shard_count, number):
    total, width = parts.shape
    rows = total // (reps * shard_count)
    bits = reps.bit_length() - 1
    widths = (halves_of(width)[0].size, halves_of(width)[1].size)
    scratch = []
    for wide in widths:
        for at in range(bits):
            scratch.append(
                pltpu.VMEM((shard_count, reps // 2 ** (at + 1), rows, wide), parts.dtype)
            )
    if shard_count > 1:
        scratch += [pltpu.VMEM((shard_count - 1, rows, wide), parts.dtype) for wide in widths]
        scratch += [pltpu.SemaphoreType.DMA((HALVES, shard_count)) for _ in range(2)]
    scratch += [pltpu.SemaphoreType.DMA((HALVES, bits)) for _ in range(4)]
    out = pl.pallas_call(
        lambda *refs: reduce_kernel(reps, shard_count, *refs),
        out_shape=jax.ShapeDtypeStruct((1, reps, rows, width), parts.dtype),
        in_specs=[pl.BlockSpec(memory_space=pltpu.VMEM)],
        out_specs=pl.BlockSpec(memory_space=pltpu.VMEM),
        scratch_shapes=scratch,
        compiler_params=pltpu.CompilerParams(
            collective_id=number, has_side_effects=True, vmem_limit_bytes=VMEM_BYTES
        ),
        cost_estimate=pl.CostEstimate(
            flops=0, bytes_accessed=32 * total * width, transcendentals=0
        ),
    )(parts.reshape(shard_count, reps, rows, width))
    return out.reshape(reps * rows, width)


def gather_shard(piece):
    return lax.all_gather(piece, "shard", axis=0, tiled=True)


def shards(
    tokens,
    doc_ids,
    routes,
    norm_in_gain,
    w_query,
    w_key,
    w_value,
    w_out,
    norm_mid_gain,
    w_router,
    w_expert_in,
    w_expert_down,
    cotangent,
):
    bf16, f32 = jnp.bfloat16, jnp.float32
    row_count, model_width = tokens.shape
    groups = HEADS // KV_HEADS
    query_cols = w_query.shape[1]
    kv_cols = w_key.shape[1]
    own_rows = w_query.shape[0]
    own_experts, ff = w_expert_down.shape[:2]
    shard_at = lax.axis_index("shard")

    small = jnp.concatenate(
        [
            w_router,
            norm_in_gain[:, None],
            norm_mid_gain[:, None],
            jnp.zeros((own_rows, PAD - EXPERTS - 2), bf16),
        ],
        axis=1,
    )
    reps, shard_count = (lax.axis_size("rep"), lax.axis_size("shard"))
    all_w = gather_all(
        jnp.concatenate([w_query, w_key, w_value, w_out, small], axis=1), reps, shard_count, 1
    )
    qkv_cols = query_cols + 2 * kv_cols
    qkv_w = all_w[:, :qkv_cols]
    out_w = all_w[:, qkv_cols : qkv_cols + w_out.shape[1]]
    small_full = all_w[:, qkv_cols + w_out.shape[1] :]
    router_full = small_full[:, :EXPERTS]
    gain_in = small_full[:, EXPERTS].astype(f32)
    gain_mid = small_full[:, EXPERTS + 1].astype(f32)
    mask_own = jnp.any(
        routes[:, :, None] == jnp.arange(EXPERTS, dtype=jnp.int32)[None, None, :], axis=1
    )
    side = jnp.concatenate(
        [cotangent, mask_own.astype(bf16), jnp.zeros((row_count, PAD - EXPERTS), bf16)], axis=1
    )
    side_all = gather_shard(side)
    dy_all = side_all[:, :model_width]
    mask_all = side_all[:, model_width : model_width + EXPERTS] > 0

    inputs = tokens.astype(f32)
    grad_final = cotangent.astype(f32)
    cosine, sine_table = rotary_tables(positions(doc_ids), HEAD_DIM)
    normed_in, scale_in = normalize(inputs)
    first_low = (normed_in * gain_in).astype(bf16)
    qkv_pre = jnp.dot(first_low, qkv_w, preferred_element_type=f32)
    query_pre = qkv_pre[:, :query_cols]
    key_pre = qkv_pre[:, query_cols : query_cols + kv_cols]
    value_pre = qkv_pre[:, query_cols + kv_cols :]
    query_rows = (
        rotate(query_pre.reshape(row_count, HEADS, HEAD_DIM), cosine, sine_table)
        .astype(bf16)
        .reshape(row_count, KV_HEADS, groups, HEAD_DIM)
    )
    key_rows = rotate(key_pre.reshape(row_count, KV_HEADS, HEAD_DIM), cosine, sine_table).astype(
        bf16
    )
    value_rows = value_pre.astype(bf16).reshape(row_count, KV_HEADS, HEAD_DIM)
    att_rows, log_sums = attend(query_rows, key_rows, value_rows, doc_ids)
    att_low = att_rows.reshape(row_count, query_cols)
    middle = inputs + jnp.dot(att_low, out_w, preferred_element_type=f32)
    normed_mid, scale_mid = normalize(middle)
    second_low = (normed_mid * gain_mid).astype(bf16)

    second_all = gather_shard(second_low)
    logits = jnp.dot(second_all, router_full, preferred_element_type=f32)
    chosen = jnp.where(mask_all, logits, masked_score)
    gate_exp = jnp.where(mask_all, jnp.exp(chosen - jnp.max(chosen, axis=1, keepdims=True)), 0.0)
    gates_all = gate_exp / jnp.sum(gate_exp, axis=1, keepdims=True)
    gates_here = lax.dynamic_slice_in_dim(gates_all, shard_at * own_experts, own_experts, axis=1)
    gates_own = lax.dynamic_slice_in_dim(gates_all, shard_at * row_count, row_count, axis=0)

    gated, grad_both, grad_gates_here = experts(
        second_all, dy_all, gates_here, w_expert_in, w_expert_down
    )
    combined = jnp.einsum("etf,efd->td", gated, w_expert_down, preferred_element_type=f32)
    combined_own = lax.psum_scatter(
        combined.astype(bf16), "shard", scatter_dimension=0, tiled=True
    )
    grad_second_here = jnp.einsum("etf,edf->td", grad_both, w_expert_in, preferred_element_type=f32)
    gate_cols = lax.dynamic_update_slice_in_dim(
        jnp.zeros((grad_gates_here.shape[0], EXPERTS), f32),
        grad_gates_here,
        shard_at * own_experts,
        axis=1,
    )
    gate_high = gate_cols.astype(bf16)
    gate_low = (gate_cols - gate_high.astype(f32)).astype(bf16)
    back_rows = jnp.concatenate(
        [
            grad_second_here.astype(bf16),
            gate_high,
            gate_low,
            jnp.zeros((gate_cols.shape[0], PAD - 2 * EXPERTS), bf16),
        ],
        axis=1,
    )
    back_own = lax.psum_scatter(back_rows, "shard", scatter_dimension=0, tiled=True)
    grad_in_here = jnp.einsum("td,etf->edf", second_all, grad_both, preferred_element_type=f32)
    grad_down_here = jnp.einsum("etf,td->efd", gated, dy_all, preferred_element_type=f32)
    expert_grads = jnp.concatenate([grad_in_here.astype(bf16), grad_down_here.astype(bf16)], axis=1)
    expert_own = reduce_all(expert_grads.reshape(-1, model_width), reps, 1, 2)
    back_own, expert_own = lax.optimization_barrier((back_own, expert_own))
    expert_own = expert_own.reshape(expert_grads.shape)
    grad_in_own = expert_own[:, :model_width].astype(f32)
    grad_down_own = expert_own[:, model_width:].astype(f32)

    mixed = (middle + combined_own.astype(f32)).astype(bf16)
    gate_back = back_own[:, model_width : model_width + 2 * EXPERTS].astype(f32)
    grad_gates = gate_back[:, :EXPERTS] + gate_back[:, EXPERTS:]
    grad_logits = (
        gates_own * (grad_gates - jnp.sum(gates_own * grad_gates, axis=1, keepdims=True))
    ).astype(bf16)
    grad_router = jnp.einsum("td,te->de", second_low, grad_logits, preferred_element_type=f32)
    grad_second = back_own[:, :model_width].astype(f32) + jnp.einsum(
        "te,de->td", grad_logits, router_full, preferred_element_type=f32
    )
    grad_mid_norm, grad_gain_mid = norm_back(grad_second, normed_mid, scale_mid, gain_mid)
    grad_middle = grad_final + grad_mid_norm
    grad_branch = grad_middle.astype(bf16)
    grad_out_w = jnp.einsum("ta,td->ad", att_low, grad_branch, preferred_element_type=f32)
    grad_att = jnp.einsum("td,ad->ta", grad_branch, out_w, preferred_element_type=f32).astype(bf16)
    grad_query_rot, grad_key_rot, grad_value_rows = attend_back(
        query_rows,
        key_rows,
        value_rows,
        doc_ids,
        log_sums,
        grad_att.reshape(row_count, KV_HEADS, groups, HEAD_DIM),
    )
    grad_query_pre = (
        unrotate(grad_query_rot.reshape(row_count, HEADS, HEAD_DIM), cosine, sine_table)
        .astype(bf16)
        .reshape(row_count, query_cols)
    )
    grad_key_pre = unrotate(grad_key_rot, cosine, sine_table).astype(bf16)
    grad_pre = jnp.concatenate(
        [
            grad_query_pre,
            grad_key_pre.reshape(row_count, kv_cols),
            grad_value_rows.astype(bf16).reshape(row_count, kv_cols),
        ],
        axis=1,
    )
    grad_qkv = jnp.einsum("td,tc->dc", first_low, grad_pre, preferred_element_type=f32)
    columns = jnp.einsum("tc,dc->td", grad_pre, qkv_w, preferred_element_type=f32)
    grad_in_norm, grad_gain_in = norm_back(columns, normed_in, scale_in, gain_in)
    grad_tokens = grad_middle + grad_in_norm

    joint = jnp.concatenate(
        [
            grad_qkv.astype(bf16),
            grad_out_w.astype(bf16),
            grad_router.astype(bf16),
            grad_gain_in.astype(bf16)[:, None],
            grad_gain_mid.astype(bf16)[:, None],
            jnp.zeros((model_width, PAD - EXPERTS - 2), bf16),
        ],
        axis=1,
    )
    joint_own = reduce_all(joint, reps, shard_count, 3).astype(f32)
    edges = [0]
    for width in (query_cols, kv_cols, kv_cols, w_out.shape[1], EXPERTS, 1, 1):
        edges.append(edges[-1] + width)
    pieces = [joint_own[:, a:b] for a, b in zip(edges[:-1], edges[1:])]
    query_own, key_own, value_own, out_own, router_own, gain_in_own, gain_mid_own = pieces
    return (
        mixed,
        grad_tokens,
        gain_in_own[:, 0],
        query_own,
        key_own,
        value_own,
        out_own,
        gain_mid_own[:, 0],
        router_own,
        grad_in_own,
        grad_down_own,
    )


def experts(rows, dy_rows, gates, in_w, down_w):
    f32, bf16 = jnp.float32, jnp.bfloat16
    both = jnp.einsum("td,edf->etf", rows, in_w, preferred_element_type=f32)
    half_width = both.shape[-1] // 2
    gate_part, up_part = (both[..., :half_width], both[..., half_width:])
    sigmoid_gate = jax.nn.sigmoid(gate_part)
    silu_gate = gate_part * sigmoid_gate
    hidden = (silu_gate * up_part).astype(bf16).astype(f32)
    back = jnp.einsum("td,efd->etf", dy_rows, down_w, preferred_element_type=f32)
    gate_cols = gates.T[:, :, None]
    grad_gates = jnp.sum(hidden * back, axis=-1).T
    gated = (hidden * gate_cols).astype(bf16)
    grad_hidden = back * gate_cols
    grad_gate = grad_hidden * up_part * sigmoid_gate * (1.0 + gate_part * (1.0 - sigmoid_gate))
    grad_both = jnp.concatenate([grad_gate, grad_hidden * silu_gate], axis=-1).astype(bf16)
    return (gated, grad_both, grad_gates)


def solution(mesh):
    in_specs = (
        P(("rep", "shard"), None),
        P(("rep", "shard")),
        P(("rep", "shard"), None),
        P("shard"),
        P("shard", None),
        P("shard", None),
        P("shard", None),
        P("shard", None),
        P("shard"),
        P("shard", None),
        P("shard", None, None),
        P("shard", None, None),
        P(("rep", "shard"), None),
    )
    out_specs = (
        P(("rep", "shard"), None),
        P(("rep", "shard"), None),
        P("shard"),
        P("shard", None),
        P("shard", None),
        P("shard", None),
        P("shard", None),
        P("shard"),
        P("shard", None),
        P("shard", None, None),
        P("shard", None, None),
    )
    return jax.shard_map(shards, mesh=mesh, in_specs=in_specs, out_specs=out_specs, check_vma=False)
```
